256 devices in a mesh: tm: 4 (over y), tile: 64 (over z, x, core).
Axes of the slice: x: 4, y: 4, z: 8, core: 2. Of those that a mesh axis runs over, the one named last changes fastest.
Arguments:
- frames: bfloat16 [4, 64, 96, 7680], P('tm', 'tile'), may hold values from -6 to 6
- first_gain: float32 [96], replicated, may hold values from 0.4 to 1.6
- first_weight: bfloat16 [27, 9216], replicated, may hold values from -0.125 to 0.125
- first_bias: float32 [96], replicated, may hold values from -3 to 3
- second_gain: float32 [96], replicated, may hold values from 0.4 to 1.6
- second_weight: bfloat16 [27, 9216], replicated, may hold values from -0.125 to 0.125
- second_bias: float32 [96], replicated, may hold values from -3 to 3
Outputs:
- encoded: bfloat16 [4, 64, 96, 7680], P('tm', 'tile')
The draws below stay inside these ranges and needn't reach their ends.
All inputs are finite; a program needn't handle non-finite values.
Results may differ from the reference program's by a relative error of at most 0.0032.
Values may be sent and summed in bfloat16 or wider, within the bound.
No kernel may reach another device: no remote copies, remote signals or barrier semaphores. Data moves between devices by JAX's collectives and lax.ppermute only.
A program may use at most 128 MiB of HBM per device.

```python
import jax
import jax.numpy as jnp
from jax import lax

C = 96
TCOLS = 8
HT = 48
WT = 160
FRAMES = 4
TILES = 64
TROWS = 8


def block_scale(own_key, dims, split, low, top_value):
    loudness, own = 1.0, jax.random.fold_in(own_key, 6)
    for axis_at, shards_of in split:
        draws = jnp.exp(jax.random.uniform(jax.random.fold_in(own, axis_at), (shards_of,), jnp.float32, low / len(split), top_value / len(split)))
        loudness = loudness * jnp.repeat(draws, dims[axis_at] // shards_of).reshape([-1 if axis == axis_at else 1 for axis in range(len(dims))])
    return loudness


def scatter_about(key, extent, scale, most, split=(), held_as=jnp.bfloat16):
    drawn = jax.random.normal(key, extent, jnp.float32) * scale
    if len(split) > 0:
        drawn = block_scale(key, extent, split, -0.22, 0.18) * drawn
    return jnp.clip(drawn, min=-most, max=most).astype(held_as)


def setup_inputs(seed: int = 0) -> dict:
    key_of = jax.random.split(jax.random.key(seed), 8)
    return {
        "frames": scatter_about(key_of[0], (FRAMES, TILES, C, HT * WT), 1.0, 6.0, ((0, 4), (1, 64))),
        "first_gain": jnp.clip(1.0 + 0.12 * jax.random.normal(key_of[1], (C,), jnp.float32), 0.4, 1.6),
        "first_weight": scatter_about(key_of[2], (27, C * C), (27 * C) ** -0.5, 0.125),
        "first_bias": scatter_about(key_of[3], (C,), 0.5, 3.0, (), jnp.float32),
        "second_gain": jnp.clip(1.0 + 0.12 * jax.random.normal(key_of[4], (C,), jnp.float32), 0.4, 1.6),
        "second_weight": scatter_about(key_of[5], (27, C * C), (27 * C) ** -0.5, 0.125),
        "second_bias": scatter_about(key_of[6], (C,), 0.5, 3.0, (), jnp.float32),
    }


eps = 1e-06

def to_frames(tiled):
    count = tiled.shape[0]
    shaped = tiled.reshape(count, TROWS, TCOLS, C, HT, WT)
    return shaped.transpose(0, 3, 1, 4, 2, 5).reshape(count, C, TROWS * HT, TCOLS * WT)

def to_tiles(whole):
    count = whole.shape[0]
    shaped = whole.reshape(count, C, TROWS, HT, TCOLS, WT)
    return shaped.transpose(0, 2, 4, 1, 3, 5).reshape(count, TROWS * TCOLS, C, HT * WT)

def unpack_kernel(weight):
    shaped = weight.reshape(3, 3, 3, C, C)
    return shaped.transpose(3, 0, 4, 1, 2).reshape(C, 3 * C, 3, 3)

def activate(field, gain):
    values = field.astype(jnp.float32)
    mean_square = lax.optimization_barrier(jnp.mean(values * values, axis=1, keepdims=True))
    scaled = values * lax.rsqrt(mean_square + eps) * gain[None, :, None, None]
    return jax.nn.silu(scaled).astype(jnp.bfloat16)

def convolve(activated, weight, bias_term):
    count = activated.shape[0]
    zeros_front = jnp.zeros((2,) + activated.shape[1:], jnp.bfloat16)
    padded = jnp.concatenate([zeros_front, activated], axis=0)
    kernel = unpack_kernel(weight).astype(jnp.float32)
    results = []
    for step in range(count):
        stacked = padded[step:step + 3].reshape(3 * C, activated.shape[2], activated.shape[3]).astype(jnp.float32)
        output = lax.conv_general_dilated(stacked[None], kernel, (1, 1), ((1, 1), (1, 1)), dimension_numbers=('NCHW', 'OIHW', 'NCHW'), precision=lax.Precision.HIGHEST)[0]
        results.append(output + bias_term[:, None, None])
    return jnp.stack(results, axis=0)

def reference(frames, first_gain, first_weight, first_bias, second_gain, second_weight, second_bias):
    whole = to_frames(frames)
    first_act = activate(whole, first_gain)
    hidden = convolve(first_act, first_weight, first_bias)
    second_act = activate(hidden, second_gain)
    result = whole.astype(jnp.float32) + convolve(second_act, second_weight, second_bias)
    return to_tiles(result.astype(jnp.bfloat16))
```

```python
import functools

import jax
import jax.numpy as jnp
import numpy as np
from jax import lax
from jax.experimental import pallas as pl
from jax.experimental.pallas import tpu as pltpu
from jax.sharding import PartitionSpec as P

C = 96
TROWS = 8
TCOLS = 8
HT = 48
WT = 160
FRAMES = 4
STRIP = HT // FRAMES
LANES = STRIP * WT
PARTS = ((0, 8), (8, 4))

PITCH = WT + 4
EXT = 2688
PLACED = 2176
INSET = 2 * PITCH + 2
QUADS = 4 * (STRIP + 4)
RIM = 768
SIDES = 256
TILE = 256

eps = 1e-06
MIB = 1024 * 1024


def call(kernel, outs, scratch, args, out_space=pltpu.VMEM, mib=8, flops=0, moved=0, **more):
    specs = [pl.BlockSpec(memory_space=space) for space, _ in args]
    arrays = [array for _, array in args]
    if not isinstance(out_space, tuple):
        out_space = (out_space,) * len(outs)
    return pl.pallas_call(
        kernel,
        out_shape=[jax.ShapeDtypeStruct(s, jnp.bfloat16) for s in outs],
        in_specs=specs,
        out_specs=[pl.BlockSpec(memory_space=space) for space in out_space],
        scratch_shapes=scratch,
        compiler_params=pltpu.CompilerParams(vmem_limit_bytes=mib * MIB),
        cost_estimate=pl.CostEstimate(flops=flops, bytes_accessed=moved, transcendentals=0),
        **more,
    )(*arrays)


def smem(*arrays):
    return [(pltpu.SMEM, a) for a in arrays]


def vmem(*arrays):
    return [(pltpu.VMEM, a) for a in arrays]


def anywhere(*arrays):
    return [(pl.ANY, a) for a in arrays]


def activated(values, gain):
    mean_square = jnp.sum(values * values, axis=0, keepdims=True) * (1.0 / C)
    scaled = values * lax.rsqrt(mean_square + eps) * gain
    half = 0.5 * scaled
    return half * jnp.tanh(half) + half


def upright(row):
    at = lax.broadcasted_iota(jnp.int32, (C, C), 0) == lax.broadcasted_iota(jnp.int32, (C, C), 1)
    return jnp.sum(jnp.where(at, row, 0.0), axis=1, keepdims=True)


def strip_at(k, me):
    return pl.multiple_of(lax.rem(me + k, FRAMES) * LANES, 128)


def frame_of(k, me):
    return lax.rem(me - k + FRAMES, FRAMES)


def run_all(copies):
    for copy in copies:
        copy.start()
    for copy in copies:
        copy.wait()


def cut_kernel(me_ref, x, m1, m2, m3, sems):
    run_all(
        [
            pltpu.make_async_copy(
                x.at[:, pl.ds(strip_at(k + 1, me_ref[0]), LANES)], out, sems.at[k]
            )
            for k, out in enumerate((m1, m2, m3))
        ]
    )


def edge_kernel(x, top, bottom, quads):
    top[...] = x[:, : 2 * WT]
    bottom[...] = x[:, (HT - 2) * WT :]
    quads[...] = jnp.zeros_like(quads)
    for i in range(HT):
        at = 4 * (i + 2)
        quads[:, at : at + 2] = x[:, (i + 1) * WT - 2 : (i + 1) * WT]
        quads[:, at + 2 : at + 4] = x[:, i * WT : i * WT + 2]


def side_kernel(me_ref, exists, x, above, below, quads, out, rows_out):
    me = me_ref[0]
    out[...] = quads[...]
    for rows, row, there in ((above, 0, exists[0]), (below, HT + 2, exists[1])):
        for i in range(2):
            at = 4 * (row + i)
            first = rows[:, i * WT : i * WT + 2]
            last = rows[:, (i + 1) * WT - 2 : (i + 1) * WT]
            out[:, at : at + 2] = jnp.where(there > 0, last, jnp.zeros_like(last))
            out[:, at + 2 : at + 4] = jnp.where(there > 0, first, jnp.zeros_like(first))
    for q in range(FRAMES):
        k = lax.rem(q - me + FRAMES, FRAMES)
        start = q * LANES
        if q == 0:
            upper = jnp.where(exists[0] > 0, above[...], jnp.zeros_like(above))
        else:
            upper = x[:, start - 2 * WT : start]
        if q == FRAMES - 1:
            lower = jnp.where(exists[1] > 0, below[...], jnp.zeros_like(below))
        else:
            lower = x[:, start + LANES : start + LANES + 2 * WT]
        rows_out[k, :, : 2 * WT] = upper
        rows_out[k, :, 2 * WT :] = lower


def rim_kernel(me_ref, exists, rows, from_left, from_right, *outs):
    me = me_ref[0]
    lane = lax.broadcasted_iota(jnp.int32, (C, SIDES), 1) % 4
    left = jnp.where(exists[2] > 0, from_left[...], jnp.zeros_like(from_left))
    right = jnp.where(exists[3] > 0, from_right[...], jnp.zeros_like(from_right))
    others = jnp.where(lane < 2, left.astype(jnp.float32), right.astype(jnp.float32))
    for k in range(FRAMES):
        strip = lax.rem(me + k, FRAMES)
        outs[k][:, : 4 * WT] = rows[k]
        mine = pltpu.roll(others, lax.rem(SIDES - 4 * STRIP * strip, SIDES), 1)
        outs[k][:, 4 * WT :] = mine[:, :128].astype(jnp.bfloat16)


def early_kernel(me_ref, gain, x, m1, m2, m3, acts, placed, held, sems):
    me = me_ref[0]
    own = x.at[:, pl.ds(strip_at(0, me), LANES)]
    copies = [
        pltpu.make_async_copy(ref, held.at[frame_of(k, me)], sems.at[k])
        for k, ref in enumerate((own, m1, m2, m3))
    ]
    run_all(copies)
    gain = upright(gain[...])
    wide = STRIP * PITCH
    for t in range(FRAMES):
        for i in range(STRIP):
            placed[t, :, i * PITCH : i * PITCH + WT] = held[t, :, i * WT : (i + 1) * WT]
        act = activated(placed[t, :, :2048].astype(jnp.float32), gain).astype(jnp.bfloat16)
        acts[t, :, INSET : INSET + wide] = act[:, :wide]


def up128(n):
    return (n + 127) // 128 * 128


class Sizes:
    def __init__(self, first, rows):
        self.hidden = up128((rows + 2) * PITCH)
        self.out = up128(rows * PITCH)
        self.ext_at = first * PITCH // 128 * 128
        self.ext = up128((first + 2) * PITCH + self.hidden) - self.ext_at
        self.placed = up128(first * PITCH + self.out) - self.ext_at
        self.held = max(self.hidden, up128(2 * PITCH + self.out))


def together(tiles, tasks):
    for n, tile in enumerate(tiles):
        tile()
        for task in tasks[n * len(tasks) // len(tiles) : (n + 1) * len(tasks) // len(tiles)]:
            task()


def block_kernel(first, rows, me_ref, exists, *refs):
    acts, placed_in, r0, r1, r2, r3, w1, w2 = refs[:8]
    outs = refs[12:16]
    ext, placed, rims, rim_acts, lifted, lifted2, parts, parts2, held, total, results, sems = refs[16:]
    size = Sizes(first, rows)
    me = me_ref[0]
    copies = [
        pltpu.make_async_copy(acts.at[:, :, pl.ds(size.ext_at, size.ext)], ext, sems.at[0]),
        pltpu.make_async_copy(
            placed_in.at[:, :, pl.ds(size.ext_at, size.placed)], placed, sems.at[1]
        ),
    ]
    for k, rim in enumerate((r0, r1, r2, r3)):
        copies.append(pltpu.make_async_copy(rim, rims.at[frame_of(k, me)], sems.at[2 + k]))
    for copy in copies:
        copy.start()
    g1, b1, g2, b2 = (upright(ref[...]) for ref in refs[8:12])
    mask = inside(first, rows, me, exists)
    for copy in copies:
        copy.wait()

    def spans(lanes):
        return [(at, min(TILE, lanes - at)) for at in range(0, lanes, TILE)]

    def lift(t):
        def rim_step():
            rim_acts[t] = activated(rims[t].astype(jnp.float32), g1).astype(jnp.bfloat16)

        def row_step(i):
            at = i * PITCH + 2 - size.ext_at
            if i < 2:
                ext[t, :, at : at + WT] = rim_acts[t, :, i * WT : (i + 1) * WT]
            if i >= STRIP + 2:
                near = (i - STRIP) * WT
                ext[t, :, at : at + WT] = rim_acts[t, :, near : near + WT]
            side = 4 * WT + 4 * i
            if i == first:
                ext[t, :, at - 2 : at] = rim_acts[t, :, side : side + 2]
            last = 2 if i == first + rows + 3 else 4
            ext[t, :, at + WT : at + WT + last] = rim_acts[t, :, side + 2 : side + 2 + last]

        def copy_step(di, at, wide):
            start = (first + di) * PITCH - size.ext_at + at
            lifted[t, di * C : (di + 1) * C, at : at + wide] = ext[t, :, start : start + wide]

        steps = [rim_step]
        steps += [functools.partial(row_step, i) for i in range(first, first + rows + 4)]
        for at, wide in spans(size.hidden):
            steps += [functools.partial(copy_step, di, at, wide) for di in range(3)]
        return steps

    def products(t, w, operand, to, lanes):
        frames = min(t + 1, 3)
        depth = frames * 3 * C

        def step(at, wide):
            tile = operand[t + 1 - frames : t + 1, :, at : at + wide].reshape(depth, wide)
            to[t % 2, :, at : at + wide] = jnp.dot(
                w[:, 9 * C - depth :], tile, preferred_element_type=jnp.float32
            )

        return [functools.partial(step, at, wide) for at, wide in spans(lanes)]

    def gathered(source, t, at, wide, lanes):
        reach = min(wide + 128, lanes - at)
        field = source[t % 2, 0:C, at : at + wide]
        for dj in (1, 2):
            part = source[t % 2, dj * C : (dj + 1) * C, at : at + reach]
            field = field + pltpu.roll(part, reach - dj, 1)[:, :wide]
        return field

    def middle(t):
        def step(at, wide):
            values = gathered(parts, t, at, wide, size.hidden) + b1
            values = activated(values, g2) * mask[:, at : at + wide]
            held[t % 2, :, at : at + wide] = values.astype(jnp.bfloat16)

        return [functools.partial(step, at, wide) for at, wide in spans(size.hidden)]

    def lift2(t):
        def step(di, at, wide):
            start = di * PITCH + at
            to = lifted2.at[t, pl.ds(di * C, C), pl.ds(at, wide)]
            to[...] = held[t % 2, :, start : start + wide]

        return [
            functools.partial(step, di, at, wide) for at, wide in spans(size.out) for di in range(3)
        ]

    def finish(t):
        def step(at, wide):
            start = first * PITCH - size.ext_at + at
            values = gathered(parts2, t, at, wide, size.out) + b2
            values = values + placed[t, :, start : start + wide].astype(jnp.float32)
            total[t % 2, :, at : at + wide] = values.astype(jnp.bfloat16)

        return [functools.partial(step, at, min(wide, size.placed - at)) for at, wide in spans(size.out)]

    def compact(t):
        def step(i):
            row = total[t % 2, :, i * PITCH : i * PITCH + WT]
            results[t, :, i * WT : (i + 1) * WT] = row

        return [functools.partial(step, i) for i in range(rows)]

    def first_products(t):
        return products(t, w1, lifted, parts, size.hidden)

    def second_products(t):
        return products(t, w2, lifted2, parts2, size.out)

    for step in lift(0):
        step()
    together(first_products(0), lift(1))
    together(first_products(1), middle(0) + lift(2))
    together(first_products(2), lift2(0) + middle(1) + lift(3))
    together(second_products(0), lift2(1) + middle(2))
    together(first_products(3), lift2(2) + finish(0))
    together(second_products(1), middle(3) + compact(0))
    together(second_products(2), lift2(3) + finish(1) + compact(1))
    together(second_products(3), finish(2) + compact(2))
    for step in finish(3) + compact(3):
        step()
    run_all(
        [
            pltpu.make_async_copy(results.at[frame_of(k, me)], outs[k], sems.at[k])
            for k in range(FRAMES)
        ]
    )


def place_kernel(me_ref, *refs):
    pieces, out, sems = refs[:-2], refs[-2], refs[-1]
    copies = []
    for part, (first, rows) in enumerate(PARTS):
        for k in range(FRAMES):
            start = pl.multiple_of(strip_at(k, me_ref[0]) + first * WT, 128)
            place = out.at[:, pl.ds(start, rows * WT)]
            n = part * FRAMES + k
            copies.append(pltpu.make_async_copy(pieces[n], place, sems.at[n]))
    run_all(copies)


def weight_kernel(first, second, first_out, second_out):
    for ref, out in ((first, first_out), (second, second_out)):
        for dj in range(3):
            for n in range(9):
                out[dj * C : (dj + 1) * C, n * C : (n + 1) * C] = ref[n * 3 + dj]


def over_time(array, by):
    pairs = [(i, (i + by) % FRAMES) for i in range(FRAMES)]
    return lax.ppermute(array, "tm", pairs)


def over_tiles(array, down, right):
    pairs = [
        (i * TCOLS + j, (i + down) % TROWS * TCOLS + (j + right) % TCOLS)
        for i in range(TROWS)
        for j in range(TCOLS)
    ]
    return lax.ppermute(array, "tile", pairs)


def inside(first, rows, me, exists):
    lane = lax.broadcasted_iota(jnp.int32, (1, Sizes(first, rows).hidden), 1)
    outside = jnp.zeros(lane.shape, jnp.int32)
    if first == 0:
        absent = jnp.where(jnp.logical_or(me > 0, exists[0] > 0), 0, 1)
        outside += jnp.where(lane < PITCH, absent, 0)
    if first + rows == STRIP:
        absent = jnp.where(jnp.logical_or(me < FRAMES - 1, exists[1] > 0), 0, 1)
        outside += jnp.where(lane >= (rows + 1) * PITCH, absent, 0)
    for i in range(rows + 2):
        outside += jnp.where(lane == i * PITCH, 1 - exists[2], 0)
        outside += jnp.where(lane == i * PITCH + WT + 1, 1 - exists[3], 0)
    return jnp.where(outside > 0, 0.0, 1.0)


def block(first, rows, me, exists, sources, common):
    size = Sizes(first, rows)
    scratch = [
        pltpu.VMEM((FRAMES, C, size.ext), jnp.bfloat16),
        pltpu.VMEM((FRAMES, C, size.placed), jnp.bfloat16),
        pltpu.VMEM((FRAMES, C, RIM), jnp.bfloat16),
        pltpu.VMEM((FRAMES, C, RIM), jnp.bfloat16),
        pltpu.VMEM((FRAMES, 3 * C, size.hidden), jnp.bfloat16),
        pltpu.VMEM((FRAMES, 3 * C, size.out), jnp.bfloat16),
        pltpu.VMEM((2, 3 * C, size.hidden), jnp.float32),
        pltpu.VMEM((2, 3 * C, size.out), jnp.float32),
        pltpu.VMEM((2, C, size.held), jnp.bfloat16),
        pltpu.VMEM((2, C, size.out), jnp.bfloat16),
        pltpu.VMEM((FRAMES, C, rows * WT), jnp.bfloat16),
        pltpu.SemaphoreType.DMA((6,)),
    ]
    return call(
        functools.partial(block_kernel, first, rows),
        [(C, rows * WT)] * FRAMES,
        scratch,
        smem(me, exists) + anywhere(*sources) + vmem(*common),
        out_space=pl.ANY,
        flops=2 * 27 * C * C * (2 * rows + 2) * WT * 3,
        mib=28,
        moved=8 * MIB,
        name="block_%d" % first,
    )


def on_device(
    frames, first_gain, first_weight, first_bias, second_gain, second_weight, second_bias
):
    x = frames.reshape(C, HT * WT)
    at_time = lax.axis_index("tm")
    tile = lax.axis_index("tile")
    me = at_time.astype(jnp.int32).reshape(1)
    tile_row, tile_column = tile // TCOLS, tile % TCOLS
    exists = jnp.stack(
        [tile_row > 0, tile_row < TROWS - 1, tile_column > 0, tile_column < TCOLS - 1]
    ).astype(jnp.int32)
    dma = pltpu.SemaphoreType.DMA

    mains = call(
        cut_kernel,
        [(C, LANES)] * 3,
        [dma((3,))],
        smem(me) + anywhere(x),
        out_space=pl.ANY,
        moved=6 * C * LANES,
        name="cut",
    )
    mains = [over_time(main, k + 1) for k, main in enumerate(mains)]
    top, bottom, quads = call(
        edge_kernel,
        [(C, 2 * WT)] * 2 + [(C, SIDES)],
        [],
        vmem(x),
        moved=2 * C * HT * WT,
        name="edges",
    )
    above = over_tiles(bottom, 1, 0)
    below = over_tiles(top, -1, 0)
    quads, rows = call(
        side_kernel,
        [(C, SIDES), (FRAMES, C, 4 * WT)],
        [],
        smem(me, exists) + vmem(x, above, below, quads),
        moved=8 * C * SIDES,
        name="sides",
    )
    from_left = over_tiles(quads, 0, 1)
    from_right = over_tiles(quads, 0, -1)
    rims = call(
        rim_kernel,
        [(C, RIM)] * FRAMES,
        [],
        smem(me, exists) + vmem(rows, from_left, from_right),
        moved=8 * C * RIM,
        name="rims",
    )
    own_rim, me_late, first_weight, second_weight = lax.optimization_barrier(
        (rims[0], me, first_weight, second_weight)
    )
    rims = [own_rim] + [over_time(rims[k], k) for k in (1, 2, 3)]
    w1, w2 = call(
        weight_kernel,
        [(3 * C, 9 * C)] * 2,
        [],
        vmem(first_weight.reshape(27, C, C), second_weight.reshape(27, C, C)),
        moved=8 * 27 * C * C,
        name="weights",
    )
    acts, placed = call(
        early_kernel,
        [(FRAMES, C, EXT), (FRAMES, C, PLACED)],
        [pltpu.VMEM((FRAMES, C, LANES), jnp.bfloat16), dma((FRAMES,))],
        smem(me_late) + vmem(first_gain[None]) + anywhere(x, *mains),
        mib=12,
        moved=8 * MIB,
        name="early",
    )
    pieces = []
    scales = [a[None] for a in (first_gain, first_bias, second_gain, second_bias)]
    for first, rows in PARTS:
        me_block = me if not pieces else pieces[-1][1]
        outs = block(first, rows, me_block, exists, [acts, placed, *rims], [w1, w2, *scales])
        if pieces:
            outs, before = lax.optimization_barrier((outs, pieces[-1][0]))
            pieces[-1] = (before, None)
        own, me_block = lax.optimization_barrier((outs[0], me))
        pieces.append(([own] + [over_time(outs[k], -k) for k in (1, 2, 3)], me_block))
    pieces = [piece for part, _ in pieces for piece in part]
    (encoded,) = call(
        place_kernel,
        [(C, HT * WT)],
        [dma((len(pieces),))],
        smem(me) + anywhere(*pieces),
        out_space=pl.ANY,
        name="place",
    )
    return encoded.reshape(1, 1, C, HT * WT)


def solution(mesh):
    return jax.shard_map(
        on_device,
        mesh=mesh,
        in_specs=(P("tm", "tile", None, None), P(), P(), P(), P(), P(), P()),
        out_specs=P("tm", "tile", None, None),
        check_vma=False,
    )
```

```python
import functools

import jax
import jax.numpy as jnp
import numpy as np
from jax import lax
from jax.experimental import pallas as pl
from jax.experimental.pallas import tpu as pltpu
from jax.sharding import PartitionSpec as P

C = 96
TROWS = 8
TCOLS = 8
HT = 48
WT = 160
FRAMES = 4
STRIP = HT // FRAMES
LANES = STRIP * WT
PARTS = ((0, 8), (8, 4))

PITCH = WT + 4
EXT = 2688
PLACED = 2176
INSET = 2 * PITCH + 2
QUADS = 4 * (STRIP + 4)
RIM = 768
SIDES = 256
TILE = 256
LIFT = 512

eps = 1e-06
MIB = 1024 * 1024


def call(kernel, outs, scratch, args, out_space=pltpu.VMEM, mib=8, flops=0, moved=0, **more):
    specs = [pl.BlockSpec(memory_space=space) for space, _ in args]
    arrays = [array for _, array in args]
    if not isinstance(out_space, tuple):
        out_space = (out_space,) * len(outs)
    return pl.pallas_call(
        kernel,
        out_shape=[jax.ShapeDtypeStruct(s, jnp.bfloat16) for s in outs],
        in_specs=specs,
        out_specs=[pl.BlockSpec(memory_space=space) for space in out_space],
        scratch_shapes=scratch,
        compiler_params=pltpu.CompilerParams(vmem_limit_bytes=mib * MIB),
        cost_estimate=pl.CostEstimate(flops=flops, bytes_accessed=moved, transcendentals=0),
        **more,
    )(*arrays)


def smem(*arrays):
    return [(pltpu.SMEM, a) for a in arrays]


def vmem(*arrays):
    return [(pltpu.VMEM, a) for a in arrays]


def anywhere(*arrays):
    return [(pl.ANY, a) for a in arrays]


def activated(values, gain):
    mean_square = jnp.sum(values * values, axis=0, keepdims=True) * (1.0 / C)
    scaled = values * lax.rsqrt(mean_square + eps) * gain
    half = 0.5 * scaled
    return half * jnp.tanh(half) + half


def upright(row):
    at = lax.broadcasted_iota(jnp.int32, (C, C), 0) == lax.broadcasted_iota(jnp.int32, (C, C), 1)
    return jnp.sum(jnp.where(at, row, 0.0), axis=1, keepdims=True)


def strip_at(k, me):
    return pl.multiple_of(lax.rem(me + k, FRAMES) * LANES, 128)


def frame_of(k, me):
    return lax.rem(me - k + FRAMES, FRAMES)


def run_all(copies):
    for copy in copies:
        copy.start()
    for copy in copies:
        copy.wait()


def cut_kernel(me_ref, x, m1, m2, m3, sems):
    run_all(
        [
            pltpu.make_async_copy(
                x.at[:, pl.ds(strip_at(k + 1, me_ref[0]), LANES)], out, sems.at[k]
            )
            for k, out in enumerate((m1, m2, m3))
        ]
    )


def edge_kernel(x, top, bottom, quads):
    top[...] = x[:, : 2 * WT]
    bottom[...] = x[:, (HT - 2) * WT :]
    quads[...] = jnp.zeros_like(quads)
    for i in range(HT):
        at = 4 * (i + 2)
        quads[:, at : at + 2] = x[:, (i + 1) * WT - 2 : (i + 1) * WT]
        quads[:, at + 2 : at + 4] = x[:, i * WT : i * WT + 2]


def side_kernel(me_ref, exists, x, above, below, quads, out, rows_out):
    me = me_ref[0]
    out[...] = quads[...]
    for rows, row, there in ((above, 0, exists[0]), (below, HT + 2, exists[1])):
        for i in range(2):
            at = 4 * (row + i)
            first = rows[:, i * WT : i * WT + 2]
            last = rows[:, (i + 1) * WT - 2 : (i + 1) * WT]
            out[:, at : at + 2] = jnp.where(there > 0, last, jnp.zeros_like(last))
            out[:, at + 2 : at + 4] = jnp.where(there > 0, first, jnp.zeros_like(first))
    for q in range(FRAMES):
        k = lax.rem(q - me + FRAMES, FRAMES)
        start = q * LANES
        if q == 0:
            upper = jnp.where(exists[0] > 0, above[...], jnp.zeros_like(above))
        else:
            upper = x[:, start - 2 * WT : start]
        if q == FRAMES - 1:
            lower = jnp.where(exists[1] > 0, below[...], jnp.zeros_like(below))
        else:
            lower = x[:, start + LANES : start + LANES + 2 * WT]
        rows_out[k, :, : 2 * WT] = upper
        rows_out[k, :, 2 * WT :] = lower


def rim_kernel(me_ref, exists, rows, from_left, from_right, *outs):
    me = me_ref[0]
    lane = lax.broadcasted_iota(jnp.int32, (C, SIDES), 1) % 4
    left = jnp.where(exists[2] > 0, from_left[...], jnp.zeros_like(from_left))
    right = jnp.where(exists[3] > 0, from_right[...], jnp.zeros_like(from_right))
    others = jnp.where(lane < 2, left.astype(jnp.float32), right.astype(jnp.float32))
    for k in range(FRAMES):
        strip = lax.rem(me + k, FRAMES)
        outs[k][:, : 4 * WT] = rows[k]
        mine = pltpu.roll(others, lax.rem(SIDES - 4 * STRIP * strip, SIDES), 1)
        outs[k][:, 4 * WT :] = mine[:, :128].astype(jnp.bfloat16)


def early_kernel(me_ref, gain, x, m1, m2, m3, acts, placed, held, sems):
    me = me_ref[0]
    own = x.at[:, pl.ds(strip_at(0, me), LANES)]
    copies = [
        pltpu.make_async_copy(ref, held.at[frame_of(k, me)], sems.at[k])
        for k, ref in enumerate((own, m1, m2, m3))
    ]
    run_all(copies)
    gain = upright(gain[...])
    wide = STRIP * PITCH
    for t in range(FRAMES):
        for i in range(STRIP):
            placed[t, :, i * PITCH : i * PITCH + WT] = held[t, :, i * WT : (i + 1) * WT]
        act = activated(placed[t, :, :2048].astype(jnp.float32), gain).astype(jnp.bfloat16)
        acts[t, :, INSET : INSET + wide] = act[:, :wide]


def up128(n):
    return (n + 127) // 128 * 128


class Sizes:
    def __init__(self, first, rows):
        self.hidden = up128((rows + 2) * PITCH)
        self.out = up128(rows * PITCH)
        self.ext_at = first * PITCH // 128 * 128
        self.ext = up128((first + 2) * PITCH + self.hidden) - self.ext_at
        self.held = max(self.hidden, up128(2 * PITCH + self.out))


def together(tiles, tasks):
    for n, tile in enumerate(tiles):
        tile()
        for task in tasks[n * len(tasks) // len(tiles) : (n + 1) * len(tasks) // len(tiles)]:
            task()


def block_kernel(first, rows, me_ref, exists, *refs):
    placed, acts, r0, r1, r2, r3, w1, w2 = refs[:8]
    outs = refs[12:16]
    ext, rims, rim_acts, lifted, lifted2, parts, parts2, held, total, results, sems = refs[16:]
    size = Sizes(first, rows)
    me = me_ref[0]
    copies = [pltpu.make_async_copy(acts.at[:, :, pl.ds(size.ext_at, size.ext)], ext, sems.at[0])]
    for k, rim in enumerate((r0, r1, r2, r3)):
        copies.append(pltpu.make_async_copy(rim, rims.at[frame_of(k, me)], sems.at[1 + k]))
    for copy in copies:
        copy.start()
    g1, b1, g2, b2 = (upright(ref[...]) for ref in refs[8:12])
    mask = inside(first, rows, me, exists)
    for copy in copies:
        copy.wait()

    def spans(lanes, step=TILE):
        return [(at, min(step, lanes - at)) for at in range(0, lanes, step)]

    def lift(t):
        def rim_step():
            rim_acts[t] = activated(rims[t].astype(jnp.float32), g1).astype(jnp.bfloat16)

        def row_step(i):
            at = i * PITCH + 2 - size.ext_at
            if i < 2:
                ext[t, :, at : at + WT] = rim_acts[t, :, i * WT : (i + 1) * WT]
            if i >= STRIP + 2:
                near = (i - STRIP) * WT
                ext[t, :, at : at + WT] = rim_acts[t, :, near : near + WT]
            side = 4 * WT + 4 * i
            if i == first:
                ext[t, :, at - 2 : at] = rim_acts[t, :, side : side + 2]
            last = 2 if i == first + rows + 3 else 4
            ext[t, :, at + WT : at + WT + last] = rim_acts[t, :, side + 2 : side + 2 + last]

        def copy_step(di, at, wide):
            start = (first + di) * PITCH - size.ext_at + at
            lifted[t, di * C : (di + 1) * C, at : at + wide] = ext[t, :, start : start + wide]

        steps = [rim_step]
        steps += [functools.partial(row_step, i) for i in range(first, first + rows + 4)]
        for at, wide in spans(size.hidden, LIFT):
            steps += [functools.partial(copy_step, di, at, wide) for di in range(3)]
        return steps

    def products(t, w, operand, to, lanes):
        frames = min(t + 1, 3)
        depth = frames * 3 * C

        def step(at, wide):
            tile = operand[t + 1 - frames : t + 1, :, at : at + wide].reshape(depth, wide)
            to[t % 2, :, at : at + wide] = jnp.dot(
                w[:, 9 * C - depth :], tile, preferred_element_type=jnp.float32
            )

        return [functools.partial(step, at, wide) for at, wide in spans(lanes)]

    lane = lax.broadcasted_iota(jnp.int32, (C, 128), 1)

    def gathered(source, t, lanes):
        moved = {}

        def turned(dj, at):
            if (dj, at) not in moved:
                part = source[t % 2, dj * C : (dj + 1) * C, at : at + 128]
                moved[dj, at] = pltpu.roll(part, 128 - dj, 1)
            return moved[dj, at]

        def block(at):
            field = source[t % 2, 0:C, at : at + 128]
            after = at + 128 if at + 128 < lanes else at
            for dj in (1, 2):
                field = field + jnp.where(lane < 128 - dj, turned(dj, at), turned(dj, after))
            return field

        return block

    def middle(t):
        block = gathered(parts, t, size.hidden)

        def step(at, wide):
            values = activated(block(at) + b1, g2) * mask[:, at : at + wide]
            held[t % 2, :, at : at + wide] = values.astype(jnp.bfloat16)

        return [functools.partial(step, at, wide) for at, wide in spans(size.hidden, 128)]

    def lift2(t):
        def step(di, at, wide):
            start = di * PITCH + at
            to = lifted2.at[t, pl.ds(di * C, C), pl.ds(at, wide)]
            to[...] = held[t % 2, :, start : start + wide]

        return [
            functools.partial(step, di, at, wide)
            for at, wide in spans(size.out, LIFT)
            for di in range(3)
        ]

    def finish(t):
        block = gathered(parts2, t, size.out)

        def step(at, wide):
            start = first * PITCH + at
            values = block(at) + b2
            values = values + placed[t, :, start : start + wide].astype(jnp.float32)
            total[t % 2, :, at : at + wide] = values.astype(jnp.bfloat16)

        return [functools.partial(step, at, wide) for at, wide in spans(size.out, 128)]

    def compact(t):
        def step(i):
            row = total[t % 2, :, i * PITCH : i * PITCH + WT]
            results[t, :, i * WT : (i + 1) * WT] = row

        return [functools.partial(step, i) for i in range(rows)]

    def first_products(t):
        return products(t, w1, lifted, parts, size.hidden)

    def second_products(t):
        return products(t, w2, lifted2, parts2, size.out)

    def send(t):
        for k in range(FRAMES):

            @pl.when(frame_of(k, me) == t)
            def _():
                pltpu.make_async_copy(results.at[t], outs[k], sems.at[k]).start()

    for step in lift(0):
        step()
    together(first_products(0), lift(1))
    together(first_products(1), middle(0) + lift(2))
    together(first_products(2), lift2(0) + middle(1) + lift(3))
    together(second_products(0), lift2(1) + middle(2))
    together(first_products(3), lift2(2) + finish(0))
    together(second_products(1), middle(3) + compact(0))
    send(0)
    together(second_products(2), lift2(3) + finish(1) + compact(1))
    send(1)
    tiles, tail = second_products(3), finish(3)
    ready = min(6, len(tiles) - 1)
    together(tiles[:3], finish(2) + compact(2))
    together(tiles[3:], tail[: 2 * ready - 1] if len(tiles) > 3 else [])
    for step in (tail[2 * ready - 1 :] if len(tiles) > 3 else tail) + compact(3):
        step()
    send(2)
    send(3)
    for k in range(FRAMES):
        pltpu.make_async_copy(results.at[0], outs[k], sems.at[k]).wait()


def place_kernel(first, rows, me_ref, *refs):
    pieces, out, sems = refs[:FRAMES], refs[-2], refs[-1]
    copies = []
    for k in range(FRAMES):
        start = pl.multiple_of(strip_at(k, me_ref[0]) + first * WT, 128)
        place = out.at[:, pl.ds(start, rows * WT)]
        copies.append(pltpu.make_async_copy(pieces[k], place, sems.at[k]))
    run_all(copies)


def weight_kernel(first, second, first_out, second_out):
    for ref, out in ((first, first_out), (second, second_out)):
        for dj in range(3):
            for n in range(9):
                out[dj * C : (dj + 1) * C, n * C : (n + 1) * C] = ref[n * 3 + dj]


def over_time(array, by):
    pairs = [(i, (i + by) % FRAMES) for i in range(FRAMES)]
    return lax.ppermute(array, "tm", pairs)


def over_tiles(array, down, right):
    pairs = [
        (i * TCOLS + j, (i + down) % TROWS * TCOLS + (j + right) % TCOLS)
        for i in range(TROWS)
        for j in range(TCOLS)
    ]
    return lax.ppermute(array, "tile", pairs)


def inside(first, rows, me, exists):
    lane = lax.broadcasted_iota(jnp.int32, (1, Sizes(first, rows).hidden), 1)
    outside = jnp.zeros(lane.shape, jnp.int32)
    if first == 0:
        absent = jnp.where(jnp.logical_or(me > 0, exists[0] > 0), 0, 1)
        outside += jnp.where(lane < PITCH, absent, 0)
    if first + rows == STRIP:
        absent = jnp.where(jnp.logical_or(me < FRAMES - 1, exists[1] > 0), 0, 1)
        outside += jnp.where(lane >= (rows + 1) * PITCH, absent, 0)
    for i in range(rows + 2):
        outside += jnp.where(lane == i * PITCH, 1 - exists[2], 0)
        outside += jnp.where(lane == i * PITCH + WT + 1, 1 - exists[3], 0)
    return jnp.where(outside > 0, 0.0, 1.0)


def block(first, rows, me, exists, placed, sources, common):
    size = Sizes(first, rows)
    scratch = [
        pltpu.VMEM((FRAMES, C, size.ext), jnp.bfloat16),
        pltpu.VMEM((FRAMES, C, RIM), jnp.bfloat16),
        pltpu.VMEM((FRAMES, C, RIM), jnp.bfloat16),
        pltpu.VMEM((FRAMES, 3 * C, size.hidden), jnp.bfloat16),
        pltpu.VMEM((FRAMES, 3 * C, size.out), jnp.bfloat16),
        pltpu.VMEM((2, 3 * C, size.hidden), jnp.float32),
        pltpu.VMEM((2, 3 * C, size.out), jnp.float32),
        pltpu.VMEM((2, C, size.held), jnp.bfloat16),
        pltpu.VMEM((2, C, size.out), jnp.bfloat16),
        pltpu.VMEM((FRAMES, C, rows * WT), jnp.bfloat16),
        pltpu.SemaphoreType.DMA((5,)),
    ]
    return call(
        functools.partial(block_kernel, first, rows),
        [(C, rows * WT)] * FRAMES,
        scratch,
        smem(me, exists) + vmem(placed) + anywhere(*sources) + vmem(*common),
        out_space=pl.ANY,
        flops=2 * 27 * C * C * (2 * rows + 2) * WT * 3,
        mib=28,
        moved=8 * MIB,
        name="block_%d" % first,
    )


def on_device(
    frames, first_gain, first_weight, first_bias, second_gain, second_weight, second_bias
):
    x = frames.reshape(C, HT * WT)
    at_time = lax.axis_index("tm")
    tile = lax.axis_index("tile")
    me = at_time.astype(jnp.int32).reshape(1)
    tile_row, tile_column = tile // TCOLS, tile % TCOLS
    exists = jnp.stack(
        [tile_row > 0, tile_row < TROWS - 1, tile_column > 0, tile_column < TCOLS - 1]
    ).astype(jnp.int32)
    dma = pltpu.SemaphoreType.DMA

    top, bottom, quads = call(
        edge_kernel,
        [(C, 2 * WT)] * 2 + [(C, SIDES)],
        [],
        vmem(x),
        moved=2 * C * HT * WT,
        name="edges",
    )
    top, bottom, me_cut = lax.optimization_barrier((top, bottom, me))
    mains = call(
        cut_kernel,
        [(C, LANES)] * 3,
        [dma((3,))],
        smem(me_cut) + anywhere(x),
        out_space=pl.ANY,
        moved=6 * C * LANES,
        name="cut",
    )
    mains = [over_time(main, k + 1) for k, main in enumerate(mains)]
    above = over_tiles(bottom, 1, 0)
    below = over_tiles(top, -1, 0)
    quads, rows = call(
        side_kernel,
        [(C, SIDES), (FRAMES, C, 4 * WT)],
        [],
        smem(me, exists) + vmem(x, above, below, quads),
        moved=8 * C * SIDES,
        name="sides",
    )
    from_left = over_tiles(quads, 0, 1)
    from_right = over_tiles(quads, 0, -1)
    rims = call(
        rim_kernel,
        [(C, RIM)] * FRAMES,
        [],
        smem(me, exists) + vmem(rows, from_left, from_right),
        moved=8 * C * RIM,
        name="rims",
    )
    own_rim, me_late, first_weight, second_weight = lax.optimization_barrier(
        (rims[0], me, first_weight, second_weight)
    )
    rims = [own_rim] + [over_time(rims[k], k) for k in (1, 2, 3)]
    w1, w2 = call(
        weight_kernel,
        [(3 * C, 9 * C)] * 2,
        [],
        vmem(first_weight.reshape(27, C, C), second_weight.reshape(27, C, C)),
        moved=8 * 27 * C * C,
        name="weights",
    )
    acts, placed = call(
        early_kernel,
        [(FRAMES, C, EXT), (FRAMES, C, PLACED)],
        [pltpu.VMEM((FRAMES, C, LANES), jnp.bfloat16), dma((FRAMES,))],
        smem(me_late) + vmem(first_gain[None]) + anywhere(x, *mains),
        mib=12,
        moved=8 * MIB,
        name="early",
    )
    scales = [a[None] for a in (first_gain, first_bias, second_gain, second_bias)]
    pieces = []
    me_block = me
    for first, rows in PARTS:
        outs = block(first, rows, me_block, exists, placed, [acts, *rims], [w1, w2, *scales])
        own, me_block = lax.optimization_barrier((outs[0], me))
        pieces.append([own] + [over_time(outs[k], -k) for k in (1, 2, 3)])
    encoded = []
    for (first, rows), part in zip(PARTS, pieces):
        encoded = call(
            functools.partial(place_kernel, first, rows),
            [(C, HT * WT)],
            [dma((FRAMES,))],
            smem(me) + anywhere(*part, *encoded),
            out_space=pl.ANY,
            input_output_aliases={1 + FRAMES: 0} if encoded else {},
            name="place_%d" % first,
        )
    (encoded,) = encoded
    return encoded.reshape(1, 1, C, HT * WT)


def solution(mesh):
    return jax.shard_map(
        on_device,
        mesh=mesh,
        in_specs=(P("tm", "tile", None, None), P(), P(), P(), P(), P(), P()),
        out_specs=P("tm", "tile", None, None),
        check_vma=False,
    )
```

```python
import functools

import jax
import jax.numpy as jnp
import numpy as np
from jax import lax
from jax.experimental import pallas as pl
from jax.experimental.pallas import tpu as pltpu
from jax.sharding import PartitionSpec as P

C = 96
TROWS = 8
TCOLS = 8
HT = 48
WT = 160
FRAMES = 4
STRIP = HT // FRAMES
LANES = STRIP * WT
PARTS = ((0, 8), (8, 4))

PITCH = WT + 4
EXT = 2688
PLACED = 2176
INSET = 2 * PITCH + 2
QUADS = 4 * (STRIP + 4)
RIM = 768
SIDES = 256
TILE = 256
LIFT = 1024
CARRY = 384

eps = 1e-06
MIB = 1024 * 1024


def call(kernel, outs, scratch, args, out_space=pltpu.VMEM, mib=8, flops=0, moved=0, **more):
    specs = [pl.BlockSpec(memory_space=space) for space, _ in args]
    arrays = [array for _, array in args]
    if not isinstance(out_space, tuple):
        out_space = (out_space,) * len(outs)
    return pl.pallas_call(
        kernel,
        out_shape=[jax.ShapeDtypeStruct(s, jnp.bfloat16) for s in outs],
        in_specs=specs,
        out_specs=[pl.BlockSpec(memory_space=space) for space in out_space],
        scratch_shapes=scratch,
        compiler_params=pltpu.CompilerParams(vmem_limit_bytes=mib * MIB),
        cost_estimate=pl.CostEstimate(flops=flops, bytes_accessed=moved, transcendentals=0),
        **more,
    )(*arrays)


def smem(*arrays):
    return [(pltpu.SMEM, a) for a in arrays]


def vmem(*arrays):
    return [(pltpu.VMEM, a) for a in arrays]


def anywhere(*arrays):
    return [(pl.ANY, a) for a in arrays]


def activated(values, gain):
    mean_square = jnp.sum(values * values, axis=0, keepdims=True) * (1.0 / C)
    scaled = values * lax.rsqrt(mean_square + eps) * gain
    half = 0.5 * scaled
    return half * jnp.tanh(half) + half


def upright(row):
    at = lax.broadcasted_iota(jnp.int32, (C, C), 0) == lax.broadcasted_iota(jnp.int32, (C, C), 1)
    return jnp.sum(jnp.where(at, row, 0.0), axis=1, keepdims=True)


def strip_at(k, me):
    return pl.multiple_of(lax.rem(me + k, FRAMES) * LANES, 128)


def frame_of(k, me):
    return lax.rem(me - k + FRAMES, FRAMES)


def run_all(copies):
    for copy in copies:
        copy.start()
    for copy in copies:
        copy.wait()


def cut_kernel(me_ref, x, m1, m2, m3, sems):
    run_all(
        [
            pltpu.make_async_copy(
                x.at[:, pl.ds(strip_at(k + 1, me_ref[0]), LANES)], out, sems.at[k]
            )
            for k, out in enumerate((m1, m2, m3))
        ]
    )


def edge_kernel(x, top, bottom, quads):
    top[...] = x[:, : 2 * WT]
    bottom[...] = x[:, (HT - 2) * WT :]
    quads[...] = jnp.zeros_like(quads)
    for i in range(HT):
        at = 4 * (i + 2)
        quads[:, at : at + 2] = x[:, (i + 1) * WT - 2 : (i + 1) * WT]
        quads[:, at + 2 : at + 4] = x[:, i * WT : i * WT + 2]


def side_kernel(me_ref, exists, x, above, below, quads, out, rows_out):
    me = me_ref[0]
    out[...] = quads[...]
    for rows, row, there in ((above, 0, exists[0]), (below, HT + 2, exists[1])):
        for i in range(2):
            at = 4 * (row + i)
            first = rows[:, i * WT : i * WT + 2]
            last = rows[:, (i + 1) * WT - 2 : (i + 1) * WT]
            out[:, at : at + 2] = jnp.where(there > 0, last, jnp.zeros_like(last))
            out[:, at + 2 : at + 4] = jnp.where(there > 0, first, jnp.zeros_like(first))
    for q in range(FRAMES):
        k = lax.rem(q - me + FRAMES, FRAMES)
        start = q * LANES
        if q == 0:
            upper = jnp.where(exists[0] > 0, above[...], jnp.zeros_like(above))
        else:
            upper = x[:, start - 2 * WT : start]
        if q == FRAMES - 1:
            lower = jnp.where(exists[1] > 0, below[...], jnp.zeros_like(below))
        else:
            lower = x[:, start + LANES : start + LANES + 2 * WT]
        rows_out[k, :, : 2 * WT] = upper
        rows_out[k, :, 2 * WT :] = lower


def rim_kernel(me_ref, exists, rows, from_left, from_right, *outs):
    me = me_ref[0]
    lane = lax.broadcasted_iota(jnp.int32, (C, SIDES), 1) % 4
    left = jnp.where(exists[2] > 0, from_left[...], jnp.zeros_like(from_left))
    right = jnp.where(exists[3] > 0, from_right[...], jnp.zeros_like(from_right))
    others = jnp.where(lane < 2, left.astype(jnp.float32), right.astype(jnp.float32))
    for k in range(FRAMES):
        strip = lax.rem(me + k, FRAMES)
        outs[k][:, : 4 * WT] = rows[k]
        mine = pltpu.roll(others, lax.rem(SIDES - 4 * STRIP * strip, SIDES), 1)
        outs[k][:, 4 * WT :] = mine[:, :128].astype(jnp.bfloat16)


def early_kernel(me_ref, gain, x, m1, m2, m3, acts, placed, held, sems):
    me = me_ref[0]
    own = x.at[:, pl.ds(strip_at(0, me), LANES)]
    copies = [
        pltpu.make_async_copy(ref, held.at[frame_of(k, me)], sems.at[k])
        for k, ref in enumerate((own, m1, m2, m3))
    ]
    run_all(copies)
    gain = upright(gain[...])
    wide = STRIP * PITCH
    for t in range(FRAMES):
        for i in range(STRIP):
            placed[t, :, i * PITCH : i * PITCH + WT] = held[t, :, i * WT : (i + 1) * WT]
        act = activated(placed[t, :, :2048].astype(jnp.float32), gain).astype(jnp.bfloat16)
        acts[t, :, INSET : INSET + wide] = act[:, :wide]


def up128(n):
    return (n + 127) // 128 * 128


class Sizes:
    def __init__(self, first, rows):
        self.taken = 2 if first else 0
        self.start = first + self.taken
        self.hidden_rows = rows + 2 - self.taken
        self.hidden = up128(self.hidden_rows * PITCH)
        self.out = up128(rows * PITCH)
        self.ext_at = self.start * PITCH // 128 * 128
        self.ext = min(up128((self.start + 2) * PITCH + self.hidden), EXT) - self.ext_at
        self.held_new = CARRY if first else 0
        self.held_at = self.held_new - self.taken * PITCH
        self.held = up128(
            max(self.held_new + self.hidden, self.held_at + 2 * PITCH + self.out)
        )


def together(tiles, tasks):
    for n, tile in enumerate(tiles):
        tile()
        for task in tasks[n * len(tasks) // len(tiles) : (n + 1) * len(tasks) // len(tiles)]:
            task()


def block_kernel(first, rows, me_ref, exists, *refs):
    placed, acts, r0, r1, r2, r3, w1, w2 = refs[:8]
    outs, carry = (refs[13:17], refs[12]) if first else (refs[12:16], refs[16])
    ext, rims, rim_acts, lifted, lifted2, parts, parts2, held, total, results, sems = refs[17:]
    size = Sizes(first, rows)
    me = me_ref[0]
    copies = [pltpu.make_async_copy(acts.at[:, :, pl.ds(size.ext_at, size.ext)], ext, sems.at[0])]
    for k, rim in enumerate((r0, r1, r2, r3)):
        copies.append(pltpu.make_async_copy(rim, rims.at[frame_of(k, me)], sems.at[1 + k]))
    for copy in copies:
        copy.start()
    g1, b1, g2, b2 = (upright(ref[...]) for ref in refs[8:12])
    mask = inside(first, rows, me, exists)
    for copy in copies:
        copy.wait()

    def spans(lanes, step=TILE):
        return [(at, min(step, lanes - at)) for at in range(0, lanes, step)]

    def lift(t):
        def rim_step(at, end):
            values = activated(rims[t, :, at:end].astype(jnp.float32), g1)
            rim_acts[t, :, at:end] = values.astype(jnp.bfloat16)

        def row_step(i):
            at = i * PITCH + 2 - size.ext_at
            if i < 2:
                ext[t, :, at : at + WT] = rim_acts[t, :, i * WT : (i + 1) * WT]
            if i >= STRIP + 2:
                near = (i - STRIP) * WT
                ext[t, :, at : at + WT] = rim_acts[t, :, near : near + WT]
            side = 4 * WT + 4 * i
            if i == size.start:
                ext[t, :, at - 2 : at] = rim_acts[t, :, side : side + 2]
            last = 2 if i == first + rows + 3 else 4
            ext[t, :, at + WT : at + WT + last] = rim_acts[t, :, side + 2 : side + 2 + last]

        def copy_step(di, at, wide):
            start = (size.start + di) * PITCH - size.ext_at + at
            wide = min(wide, size.ext - start)
            lifted[t, di * C : (di + 1) * C, at : at + wide] = ext[t, :, start : start + wide]

        needed = [(0, 384), (640, RIM)] if first == 0 else [(256, RIM)]
        if first == 0 and first + rows == STRIP:
            needed = [(0, RIM)]
        steps = [functools.partial(rim_step, at, end) for at, end in needed]
        steps += [functools.partial(row_step, i) for i in range(size.start, first + rows + 4)]
        for at, wide in spans(size.hidden, LIFT):
            steps += [functools.partial(copy_step, di, at, wide) for di in range(3)]
        return steps

    def products(t, w, operand, to, lanes):
        frames = min(t + 1, 3)
        depth = frames * 3 * C

        def step(at, wide):
            tile = operand[t + 1 - frames : t + 1, :, at : at + wide].reshape(depth, wide)
            to[t % 2, :, at : at + wide] = jnp.dot(
                w[:, 9 * C - depth :], tile, preferred_element_type=jnp.float32
            )

        return [functools.partial(step, at, wide) for at, wide in spans(lanes)]

    lane = lax.broadcasted_iota(jnp.int32, (C, 128), 1)

    def gathered(source, t, lanes):
        moved = {}

        def turned(dj, at):
            if (dj, at) not in moved:
                part = source[t % 2, dj * C : (dj + 1) * C, at : at + 128]
                moved[dj, at] = pltpu.roll(part, 128 - dj, 1)
            return moved[dj, at]

        def block(at):
            field = source[t % 2, 0:C, at : at + 128]
            after = at + 128 if at + 128 < lanes else at
            for dj in (1, 2):
                field = field + jnp.where(lane < 128 - dj, turned(dj, at), turned(dj, after))
            return field

        return block

    def middle(t):
        block = gathered(parts, t, size.hidden)

        def step(at, wide):
            values = activated(block(at) + b1, g2) * mask[:, at : at + wide]
            values = values.astype(jnp.bfloat16)
            held[t % 2, :, size.held_new + at : size.held_new + at + wide] = values

        def give():
            end = size.hidden_rows * PITCH
            carry[t] = held[t % 2, :, end - CARRY : end]

        def take():
            held[t % 2, :, :CARRY] = carry[t]

        steps = [functools.partial(step, at, wide) for at, wide in spans(size.hidden, 128)]
        return [take] + steps if first else steps + [give]

    def lift2(t):
        def step(di, at, wide):
            start = size.held_at + di * PITCH + at
            to = lifted2.at[t, pl.ds(di * C, C), pl.ds(at, wide)]
            to[...] = held[t % 2, :, start : start + wide]

        return [
            functools.partial(step, di, at, wide)
            for at, wide in spans(size.out, LIFT)
            for di in range(3)
        ]

    def finish(t):
        block = gathered(parts2, t, size.out)

        def step(at, wide):
            start = first * PITCH + at
            values = block(at) + b2
            values = values + placed[t, :, start : start + wide].astype(jnp.float32)
            total[t % 2, :, at : at + wide] = values.astype(jnp.bfloat16)

        return [functools.partial(step, at, wide) for at, wide in spans(size.out, 128)]

    def compact(t):
        def step(i):
            row = total[t % 2, :, i * PITCH : i * PITCH + WT]
            results[t, :, i * WT : (i + 1) * WT] = row

        return [functools.partial(step, i) for i in range(rows)]

    def first_products(t):
        return products(t, w1, lifted, parts, size.hidden)

    def second_products(t):
        return products(t, w2, lifted2, parts2, size.out)

    def send(t):
        for k in range(FRAMES):

            @pl.when(frame_of(k, me) == t)
            def _():
                pltpu.make_async_copy(results.at[t], outs[k], sems.at[k]).start()

    for step in lift(0):
        step()
    together(first_products(0), lift(1))
    together(first_products(1), middle(0) + lift(2))
    together(first_products(2), lift2(0) + middle(1) + lift(3))
    together(second_products(0), lift2(1) + middle(2))
    together(first_products(3), lift2(2) + finish(0))
    together(second_products(1), middle(3) + compact(0))
    send(0)
    together(second_products(2), lift2(3) + finish(1) + compact(1))
    send(1)
    tiles, tail = second_products(3), finish(3)
    ready = min(6, len(tiles) - 1)
    together(tiles[:3], finish(2) + compact(2))
    together(tiles[3:], tail[: 2 * ready - 1] if len(tiles) > 3 else [])
    for step in (tail[2 * ready - 1 :] if len(tiles) > 3 else tail) + compact(3):
        step()
    send(2)
    send(3)
    for k in range(FRAMES):
        pltpu.make_async_copy(results.at[0], outs[k], sems.at[k]).wait()


def place_kernel(first, rows, me_ref, *refs):
    pieces, out, sems = refs[:FRAMES], refs[-2], refs[-1]
    copies = []
    for k in range(FRAMES):
        start = pl.multiple_of(strip_at(k, me_ref[0]) + first * WT, 128)
        place = out.at[:, pl.ds(start, rows * WT)]
        copies.append(pltpu.make_async_copy(pieces[k], place, sems.at[k]))
    run_all(copies)


def weight_kernel(first, second, first_out, second_out):
    for ref, out in ((first, first_out), (second, second_out)):
        for dj in range(3):
            for n in range(9):
                out[dj * C : (dj + 1) * C, n * C : (n + 1) * C] = ref[n * 3 + dj]


def over_time(array, by):
    pairs = [(i, (i + by) % FRAMES) for i in range(FRAMES)]
    return lax.ppermute(array, "tm", pairs)


def over_tiles(array, down, right):
    pairs = [
        (i * TCOLS + j, (i + down) % TROWS * TCOLS + (j + right) % TCOLS)
        for i in range(TROWS)
        for j in range(TCOLS)
    ]
    return lax.ppermute(array, "tile", pairs)


def inside(first, rows, me, exists):
    size = Sizes(first, rows)
    lane = lax.broadcasted_iota(jnp.int32, (1, size.hidden), 1)
    outside = jnp.zeros(lane.shape, jnp.int32)
    if first == 0:
        absent = jnp.where(jnp.logical_or(me > 0, exists[0] > 0), 0, 1)
        outside += jnp.where(lane < PITCH, absent, 0)
    if first + rows == STRIP:
        absent = jnp.where(jnp.logical_or(me < FRAMES - 1, exists[1] > 0), 0, 1)
        outside += jnp.where(lane >= (size.hidden_rows - 1) * PITCH, absent, 0)
    for i in range(size.hidden_rows):
        outside += jnp.where(lane == i * PITCH, 1 - exists[2], 0)
        outside += jnp.where(lane == i * PITCH + WT + 1, 1 - exists[3], 0)
    return jnp.where(outside > 0, 0.0, 1.0)


def block(first, rows, me, exists, placed, carry, sources, common):
    size = Sizes(first, rows)
    scratch = [
        pltpu.VMEM((FRAMES, C, size.ext), jnp.bfloat16),
        pltpu.VMEM((FRAMES, C, RIM), jnp.bfloat16),
        pltpu.VMEM((FRAMES, C, RIM), jnp.bfloat16),
        pltpu.VMEM((FRAMES, 3 * C, size.hidden), jnp.bfloat16),
        pltpu.VMEM((FRAMES, 3 * C, size.out), jnp.bfloat16),
        pltpu.VMEM((2, 3 * C, size.hidden), jnp.float32),
        pltpu.VMEM((2, 3 * C, size.out), jnp.float32),
        pltpu.VMEM((2, C, size.held), jnp.bfloat16),
        pltpu.VMEM((2, C, size.out), jnp.bfloat16),
        pltpu.VMEM((FRAMES, C, rows * WT), jnp.bfloat16),
        pltpu.SemaphoreType.DMA((5,)),
    ]
    return call(
        functools.partial(block_kernel, first, rows),
        [(C, rows * WT)] * FRAMES + ([] if first else [(FRAMES, C, CARRY)]),
        scratch,
        smem(me, exists) + vmem(placed) + anywhere(*sources) + vmem(*common, *carry),
        out_space=(pl.ANY,) * FRAMES + (() if first else (pltpu.VMEM,)),
        flops=2 * 27 * C * C * (2 * rows + 2) * WT * 3,
        mib=28,
        moved=8 * MIB,
        name="block_%d" % first,
    )


def on_device(
    frames, first_gain, first_weight, first_bias, second_gain, second_weight, second_bias
):
    x = frames.reshape(C, HT * WT)
    at_time = lax.axis_index("tm")
    tile = lax.axis_index("tile")
    me = at_time.astype(jnp.int32).reshape(1)
    tile_row, tile_column = tile // TCOLS, tile % TCOLS
    exists = jnp.stack(
        [tile_row > 0, tile_row < TROWS - 1, tile_column > 0, tile_column < TCOLS - 1]
    ).astype(jnp.int32)
    dma = pltpu.SemaphoreType.DMA

    top, bottom, quads = call(
        edge_kernel,
        [(C, 2 * WT)] * 2 + [(C, SIDES)],
        [],
        vmem(x),
        moved=2 * C * HT * WT,
        name="edges",
    )
    top, bottom, me_cut = lax.optimization_barrier((top, bottom, me))
    mains = call(
        cut_kernel,
        [(C, LANES)] * 3,
        [dma((3,))],
        smem(me_cut) + anywhere(x),
        out_space=pl.ANY,
        moved=6 * C * LANES,
        name="cut",
    )
    mains = [over_time(main, k + 1) for k, main in enumerate(mains)]
    above = over_tiles(bottom, 1, 0)
    below = over_tiles(top, -1, 0)
    quads, rows = call(
        side_kernel,
        [(C, SIDES), (FRAMES, C, 4 * WT)],
        [],
        smem(me, exists) + vmem(x, above, below, quads),
        moved=8 * C * SIDES,
        name="sides",
    )
    from_left = over_tiles(quads, 0, 1)
    from_right = over_tiles(quads, 0, -1)
    rims = call(
        rim_kernel,
        [(C, RIM)] * FRAMES,
        [],
        smem(me, exists) + vmem(rows, from_left, from_right),
        moved=8 * C * RIM,
        name="rims",
    )
    own_rim, me_late, first_weight, second_weight = lax.optimization_barrier(
        (rims[0], me, first_weight, second_weight)
    )
    rims = [own_rim] + [over_time(rims[k], k) for k in (1, 2, 3)]
    w1, w2 = call(
        weight_kernel,
        [(3 * C, 9 * C)] * 2,
        [],
        vmem(first_weight.reshape(27, C, C), second_weight.reshape(27, C, C)),
        moved=8 * 27 * C * C,
        name="weights",
    )
    acts, placed = call(
        early_kernel,
        [(FRAMES, C, EXT), (FRAMES, C, PLACED)],
        [pltpu.VMEM((FRAMES, C, LANES), jnp.bfloat16), dma((FRAMES,))],
        smem(me_late) + vmem(first_gain[None]) + anywhere(x, *mains),
        mib=12,
        moved=8 * MIB,
        name="early",
    )
    scales = [a[None] for a in (first_gain, first_bias, second_gain, second_bias)]
    pieces = []
    carry = []
    for first, rows in PARTS:
        common = [w1, w2, *scales]
        outs = block(first, rows, me, exists, placed, carry, [acts, *rims], common)
        own, *carry = lax.optimization_barrier((outs[0], *outs[FRAMES:]))
        pieces.append([own] + [over_time(outs[k], -k) for k in (1, 2, 3)])
    encoded = []
    for (first, rows), part in zip(PARTS, pieces):
        encoded = call(
            functools.partial(place_kernel, first, rows),
            [(C, HT * WT)],
            [dma((FRAMES,))],
            smem(me) + anywhere(*part, *encoded),
            out_space=pl.ANY,
            input_output_aliases={1 + FRAMES: 0} if encoded else {},
            name="place_%d" % first,
        )
    (encoded,) = encoded
    return encoded.reshape(1, 1, C, HT * WT)


def solution(mesh):
    return jax.shard_map(
        on_device,
        mesh=mesh,
        in_specs=(P("tm", "tile", None, None), P(), P(), P(), P(), P(), P()),
        out_specs=P("tm", "tile", None, None),
        check_vma=False,
    )
```

```python
import functools

import jax
import jax.numpy as jnp
import numpy as np
from jax import lax
from jax.experimental import pallas as pl
from jax.experimental.pallas import tpu as pltpu
from jax.sharding import PartitionSpec as P

C = 96
TROWS = 8
TCOLS = 8
HT = 48
WT = 160
FRAMES = 4
STRIP = HT // FRAMES
LANES = STRIP * WT
PARTS = ((0, 8), (8, 4))

PITCH = WT + 4
EXT = 2688
PLACED = 2176
INSET = 2 * PITCH + 2
QUADS = 4 * (STRIP + 4)
RIM = 768
SIDES = 256
TILE = 256
LIFT = 1024
CARRY = 384

eps = 1e-06
MIB = 1024 * 1024


def call(kernel, outs, scratch, args, out_space=pltpu.VMEM, mib=8, flops=0, moved=0, **more):
    specs = [pl.BlockSpec(memory_space=space) for space, _ in args]
    arrays = [array for _, array in args]
    if not isinstance(out_space, tuple):
        out_space = (out_space,) * len(outs)
    return pl.pallas_call(
        kernel,
        out_shape=[jax.ShapeDtypeStruct(s, jnp.bfloat16) for s in outs],
        in_specs=specs,
        out_specs=[pl.BlockSpec(memory_space=space) for space in out_space],
        scratch_shapes=scratch,
        compiler_params=pltpu.CompilerParams(vmem_limit_bytes=mib * MIB),
        cost_estimate=pl.CostEstimate(flops=flops, bytes_accessed=moved, transcendentals=0),
        **more,
    )(*arrays)


def smem(*arrays):
    return [(pltpu.SMEM, a) for a in arrays]


def vmem(*arrays):
    return [(pltpu.VMEM, a) for a in arrays]


def anywhere(*arrays):
    return [(pl.ANY, a) for a in arrays]


def activated(values, gain):
    mean_square = jnp.sum(values * values, axis=0, keepdims=True) * (1.0 / C)
    scaled = values * lax.rsqrt(mean_square + eps) * gain
    half = 0.5 * scaled
    return half * jnp.tanh(half) + half


def upright(row):
    at = lax.broadcasted_iota(jnp.int32, (C, C), 0) == lax.broadcasted_iota(jnp.int32, (C, C), 1)
    return jnp.sum(jnp.where(at, row, 0.0), axis=1, keepdims=True)


def strip_at(k, me):
    return pl.multiple_of(lax.rem(me + k, FRAMES) * LANES, 128)


def frame_of(k, me):
    return lax.rem(me - k + FRAMES, FRAMES)


def run_all(copies):
    for copy in copies:
        copy.start()
    for copy in copies:
        copy.wait()


def cut_kernel(me_ref, x, m1, m2, m3, sems):
    run_all(
        [
            pltpu.make_async_copy(
                x.at[:, pl.ds(strip_at(k + 1, me_ref[0]), LANES)], out, sems.at[k]
            )
            for k, out in enumerate((m1, m2, m3))
        ]
    )


def edge_kernel(x, top, bottom, quads):
    top[...] = x[:, : 2 * WT]
    bottom[...] = x[:, (HT - 2) * WT :]
    quads[...] = jnp.zeros_like(quads)
    for i in range(HT):
        at = 4 * (i + 2)
        quads[:, at : at + 2] = x[:, (i + 1) * WT - 2 : (i + 1) * WT]
        quads[:, at + 2 : at + 4] = x[:, i * WT : i * WT + 2]


def side_kernel(me_ref, exists, x, above, below, quads, out, rows_out):
    me = me_ref[0]
    out[...] = quads[...]
    for rows, row, there in ((above, 0, exists[0]), (below, HT + 2, exists[1])):
        for i in range(2):
            at = 4 * (row + i)
            first = rows[:, i * WT : i * WT + 2]
            last = rows[:, (i + 1) * WT - 2 : (i + 1) * WT]
            out[:, at : at + 2] = jnp.where(there > 0, last, jnp.zeros_like(last))
            out[:, at + 2 : at + 4] = jnp.where(there > 0, first, jnp.zeros_like(first))
    for q in range(FRAMES):
        k = lax.rem(q - me + FRAMES, FRAMES)
        start = q * LANES
        if q == 0:
            upper = jnp.where(exists[0] > 0, above[...], jnp.zeros_like(above))
        else:
            upper = x[:, start - 2 * WT : start]
        if q == FRAMES - 1:
            lower = jnp.where(exists[1] > 0, below[...], jnp.zeros_like(below))
        else:
            lower = x[:, start + LANES : start + LANES + 2 * WT]
        rows_out[k, :, : 2 * WT] = upper
        rows_out[k, :, 2 * WT :] = lower


def rim_kernel(me_ref, exists, rows, from_left, from_right, *outs):
    me = me_ref[0]
    lane = lax.broadcasted_iota(jnp.int32, (C, SIDES), 1) % 4
    left = jnp.where(exists[2] > 0, from_left[...], jnp.zeros_like(from_left))
    right = jnp.where(exists[3] > 0, from_right[...], jnp.zeros_like(from_right))
    others = jnp.where(lane < 2, left.astype(jnp.float32), right.astype(jnp.float32))
    for k in range(FRAMES):
        strip = lax.rem(me + k, FRAMES)
        outs[k][:, : 4 * WT] = rows[k]
        mine = pltpu.roll(others, lax.rem(SIDES - 4 * STRIP * strip, SIDES), 1)
        outs[k][:, 4 * WT :] = mine[:, :128].astype(jnp.bfloat16)


def early_kernel(me_ref, gain, x, m1, m2, m3, acts, placed, held, flat, sems):
    me = me_ref[0]
    own = x.at[:, pl.ds(strip_at(0, me), LANES)]
    copies = [
        pltpu.make_async_copy(ref, held.at[frame_of(k, me)], sems.at[k])
        for k, ref in enumerate((own, m1, m2, m3))
    ]
    run_all(copies)
    gain = upright(gain[...])
    wide = STRIP * PITCH
    for t in range(FRAMES):
        for i in range(STRIP):
            placed[t, :, i * PITCH : i * PITCH + WT] = held[t, :, i * WT : (i + 1) * WT]
        for at in range(0, 2048, 128):
            values = activated(placed[t, :, at : at + 128].astype(jnp.float32), gain)
            flat[:, at : at + 128] = values.astype(jnp.bfloat16)
        acts[t, :, INSET : INSET + wide] = flat[:, :wide]


def up128(n):
    return (n + 127) // 128 * 128


class Sizes:
    def __init__(self, first, rows):
        self.taken = 2 if first else 0
        self.start = first + self.taken
        self.hidden_rows = rows + 2 - self.taken
        self.hidden = up128(self.hidden_rows * PITCH)
        self.out = up128(rows * PITCH)
        self.ext_at = self.start * PITCH // 128 * 128
        self.ext = min(up128((self.start + 2) * PITCH + self.hidden), EXT) - self.ext_at
        self.held_new = CARRY if first else 0
        self.held_at = self.held_new - self.taken * PITCH
        self.held = up128(
            max(self.held_new + self.hidden, self.held_at + 2 * PITCH + self.out)
        )


def together(tiles, tasks):
    for n, tile in enumerate(tiles):
        tile()
        for task in tasks[n * len(tasks) // len(tiles) : (n + 1) * len(tasks) // len(tiles)]:
            task()


def block_kernel(first, rows, me_ref, exists, *refs):
    placed, acts, r0, r1, r2, r3, w1, w2 = refs[:8]
    outs, carry = (refs[13:17], refs[12]) if first else (refs[12:16], refs[16])
    ext, rims, rim_acts, lifted, lifted2, parts, parts2, held, total, results, sems = refs[17:]
    size = Sizes(first, rows)
    me = me_ref[0]
    copies = [pltpu.make_async_copy(acts.at[:, :, pl.ds(size.ext_at, size.ext)], ext, sems.at[0])]
    for k, rim in enumerate((r0, r1, r2, r3)):
        copies.append(pltpu.make_async_copy(rim, rims.at[frame_of(k, me)], sems.at[1 + k]))
    for copy in copies:
        copy.start()
    g1, b1, g2, b2 = (upright(ref[...]) for ref in refs[8:12])
    mask = inside(first, rows, me, exists)
    for copy in copies:
        copy.wait()

    def spans(lanes, step=TILE):
        return [(at, min(step, lanes - at)) for at in range(0, lanes, step)]

    def lift(t):
        def rim_step(at, end):
            values = activated(rims[t, :, at:end].astype(jnp.float32), g1)
            rim_acts[t, :, at:end] = values.astype(jnp.bfloat16)

        def row_step(i):
            at = i * PITCH + 2 - size.ext_at
            if i < 2:
                ext[t, :, at : at + WT] = rim_acts[t, :, i * WT : (i + 1) * WT]
            if i >= STRIP + 2:
                near = (i - STRIP) * WT
                ext[t, :, at : at + WT] = rim_acts[t, :, near : near + WT]
            side = 4 * WT + 4 * i
            if i == size.start:
                ext[t, :, at - 2 : at] = rim_acts[t, :, side : side + 2]
            last = 2 if i == first + rows + 3 else 4
            ext[t, :, at + WT : at + WT + last] = rim_acts[t, :, side + 2 : side + 2 + last]

        def copy_step(di, at, wide):
            start = (size.start + di) * PITCH - size.ext_at + at
            wide = min(wide, size.ext - start)
            lifted[t, di * C : (di + 1) * C, at : at + wide] = ext[t, :, start : start + wide]

        needed = [(0, 384), (640, RIM)] if first == 0 else [(256, RIM)]
        if first == 0 and first + rows == STRIP:
            needed = [(0, RIM)]
        steps = [functools.partial(rim_step, at, end) for at, end in needed]
        steps += [functools.partial(row_step, i) for i in range(size.start, first + rows + 4)]
        for at, wide in spans(size.hidden, LIFT):
            steps += [functools.partial(copy_step, di, at, wide) for di in range(3)]
        return steps

    def products(t, w, operand, to, lanes):
        frames = min(t + 1, 3)
        depth = frames * 3 * C

        def step(at, wide):
            tile = operand[t + 1 - frames : t + 1, :, at : at + wide].reshape(depth, wide)
            to[t % 2, :, at : at + wide] = jnp.dot(
                w[:, 9 * C - depth :], tile, preferred_element_type=jnp.float32
            )

        return [functools.partial(step, at, wide) for at, wide in spans(lanes)]

    lane = lax.broadcasted_iota(jnp.int32, (C, 128), 1)

    def gathered(source, t, lanes):
        moved = {}

        def turned(dj, at):
            if (dj, at) not in moved:
                part = source[t % 2, dj * C : (dj + 1) * C, at : at + 128]
                moved[dj, at] = pltpu.roll(part, 128 - dj, 1)
            return moved[dj, at]

        def block(at):
            field = source[t % 2, 0:C, at : at + 128]
            after = at + 128 if at + 128 < lanes else at
            for dj in (1, 2):
                field = field + jnp.where(lane < 128 - dj, turned(dj, at), turned(dj, after))
            return field

        return block

    def middle(t):
        block = gathered(parts, t, size.hidden)

        def step(at, wide):
            values = activated(block(at) + b1, g2) * mask[:, at : at + wide]
            values = values.astype(jnp.bfloat16)
            held[t % 2, :, size.held_new + at : size.held_new + at + wide] = values

        def give():
            end = size.hidden_rows * PITCH
            carry[t] = held[t % 2, :, end - CARRY : end]

        def take():
            held[t % 2, :, :CARRY] = carry[t]

        steps = [functools.partial(step, at, wide) for at, wide in spans(size.hidden, 128)]
        return [take] + steps if first else steps + [give]

    def lift2(t):
        def step(di, at, wide):
            start = size.held_at + di * PITCH + at
            to = lifted2.at[t, pl.ds(di * C, C), pl.ds(at, wide)]
            to[...] = held[t % 2, :, start : start + wide]

        return [
            functools.partial(step, di, at, wide)
            for at, wide in spans(size.out, LIFT)
            for di in range(3)
        ]

    def finish(t):
        block = gathered(parts2, t, size.out)

        def step(at, wide):
            start = first * PITCH + at
            values = block(at) + b2
            values = values + placed[t, :, start : start + wide].astype(jnp.float32)
            total[t % 2, :, at : at + wide] = values.astype(jnp.bfloat16)

        return [functools.partial(step, at, wide) for at, wide in spans(size.out, 128)]

    def compact(t):
        def step(i):
            row = total[t % 2, :, i * PITCH : i * PITCH + WT]
            results[t, :, i * WT : (i + 1) * WT] = row

        return [functools.partial(step, i) for i in range(rows)]

    def first_products(t):
        return products(t, w1, lifted, parts, size.hidden)

    def second_products(t):
        return products(t, w2, lifted2, parts2, size.out)

    def send(t):
        for k in range(FRAMES):

            @pl.when(frame_of(k, me) == t)
            def _():
                pltpu.make_async_copy(results.at[t], outs[k], sems.at[k]).start()

    for step in lift(0):
        step()
    together(first_products(0), lift(1))
    together(first_products(1), middle(0) + lift(2))
    together(first_products(2), lift2(0) + middle(1) + lift(3))
    together(second_products(0), lift2(1) + middle(2))
    together(first_products(3), lift2(2) + finish(0))
    together(second_products(1), middle(3) + compact(0))
    send(0)
    together(second_products(2), lift2(3) + finish(1) + compact(1))
    send(1)
    tiles, tail = second_products(3), finish(3)
    ready = min(6, len(tiles) - 1)
    together(tiles[:3], finish(2) + compact(2))
    together(tiles[3:], tail[: 2 * ready - 1] if len(tiles) > 3 else [])
    for step in (tail[2 * ready - 1 :] if len(tiles) > 3 else tail) + compact(3):
        step()
    send(2)
    send(3)
    for k in range(FRAMES):
        pltpu.make_async_copy(results.at[0], outs[k], sems.at[k]).wait()


def place_kernel(first, rows, me_ref, *refs):
    pieces, out, sems = refs[:FRAMES], refs[-2], refs[-1]
    copies = []
    for k in range(FRAMES):
        start = pl.multiple_of(strip_at(k, me_ref[0]) + first * WT, 128)
        place = out.at[:, pl.ds(start, rows * WT)]
        copies.append(pltpu.make_async_copy(pieces[k], place, sems.at[k]))
    run_all(copies)


def weight_kernel(first, second, first_out, second_out):
    for ref, out in ((first, first_out), (second, second_out)):
        for dj in range(3):
            for n in range(9):
                out[dj * C : (dj + 1) * C, n * C : (n + 1) * C] = ref[n * 3 + dj]


def over_time(array, by):
    pairs = [(i, (i + by) % FRAMES) for i in range(FRAMES)]
    return lax.ppermute(array, "tm", pairs)


def over_tiles(array, down, right):
    pairs = [
        (i * TCOLS + j, (i + down) % TROWS * TCOLS + (j + right) % TCOLS)
        for i in range(TROWS)
        for j in range(TCOLS)
    ]
    return lax.ppermute(array, "tile", pairs)


def inside(first, rows, me, exists):
    size = Sizes(first, rows)
    lane = lax.broadcasted_iota(jnp.int32, (1, size.hidden), 1)
    outside = jnp.zeros(lane.shape, jnp.int32)
    if first == 0:
        absent = jnp.where(jnp.logical_or(me > 0, exists[0] > 0), 0, 1)
        outside += jnp.where(lane < PITCH, absent, 0)
    if first + rows == STRIP:
        absent = jnp.where(jnp.logical_or(me < FRAMES - 1, exists[1] > 0), 0, 1)
        outside += jnp.where(lane >= (size.hidden_rows - 1) * PITCH, absent, 0)
    for i in range(size.hidden_rows):
        outside += jnp.where(lane == i * PITCH, 1 - exists[2], 0)
        outside += jnp.where(lane == i * PITCH + WT + 1, 1 - exists[3], 0)
    return jnp.where(outside > 0, 0.0, 1.0)


def block(first, rows, me, exists, placed, carry, sources, common):
    size = Sizes(first, rows)
    scratch = [
        pltpu.VMEM((FRAMES, C, size.ext), jnp.bfloat16),
        pltpu.VMEM((FRAMES, C, RIM), jnp.bfloat16),
        pltpu.VMEM((FRAMES, C, RIM), jnp.bfloat16),
        pltpu.VMEM((FRAMES, 3 * C, size.hidden), jnp.bfloat16),
        pltpu.VMEM((FRAMES, 3 * C, size.out), jnp.bfloat16),
        pltpu.VMEM((2, 3 * C, size.hidden), jnp.float32),
        pltpu.VMEM((2, 3 * C, size.out), jnp.float32),
        pltpu.VMEM((2, C, size.held), jnp.bfloat16),
        pltpu.VMEM((2, C, size.out), jnp.bfloat16),
        pltpu.VMEM((FRAMES, C, rows * WT), jnp.bfloat16),
        pltpu.SemaphoreType.DMA((5,)),
    ]
    return call(
        functools.partial(block_kernel, first, rows),
        [(C, rows * WT)] * FRAMES + ([] if first else [(FRAMES, C, CARRY)]),
        scratch,
        smem(me, exists) + vmem(placed) + anywhere(*sources) + vmem(*common, *carry),
        out_space=(pl.ANY,) * FRAMES + (() if first else (pltpu.VMEM,)),
        flops=2 * 27 * C * C * (2 * rows + 2) * WT * 3,
        mib=28,
        moved=8 * MIB,
        name="block_%d" % first,
    )


def on_device(
    frames, first_gain, first_weight, first_bias, second_gain, second_weight, second_bias
):
    x = frames.reshape(C, HT * WT)
    at_time = lax.axis_index("tm")
    tile = lax.axis_index("tile")
    me = at_time.astype(jnp.int32).reshape(1)
    tile_row, tile_column = tile // TCOLS, tile % TCOLS
    exists = jnp.stack(
        [tile_row > 0, tile_row < TROWS - 1, tile_column > 0, tile_column < TCOLS - 1]
    ).astype(jnp.int32)
    dma = pltpu.SemaphoreType.DMA

    top, bottom, quads = call(
        edge_kernel,
        [(C, 2 * WT)] * 2 + [(C, SIDES)],
        [],
        vmem(x),
        moved=2 * C * HT * WT,
        name="edges",
    )
    top, bottom, me_cut = lax.optimization_barrier((top, bottom, me))
    mains = call(
        cut_kernel,
        [(C, LANES)] * 3,
        [dma((3,))],
        smem(me_cut) + anywhere(x),
        out_space=pl.ANY,
        moved=6 * C * LANES,
        name="cut",
    )
    mains = [over_time(main, k + 1) for k, main in enumerate(mains)]
    above = over_tiles(bottom, 1, 0)
    below = over_tiles(top, -1, 0)
    quads, rows = call(
        side_kernel,
        [(C, SIDES), (FRAMES, C, 4 * WT)],
        [],
        smem(me, exists) + vmem(x, above, below, quads),
        moved=8 * C * SIDES,
        name="sides",
    )
    from_left = over_tiles(quads, 0, 1)
    from_right = over_tiles(quads, 0, -1)
    rims = call(
        rim_kernel,
        [(C, RIM)] * FRAMES,
        [],
        smem(me, exists) + vmem(rows, from_left, from_right),
        moved=8 * C * RIM,
        name="rims",
    )
    own_rim, me_late, first_weight, second_weight = lax.optimization_barrier(
        (rims[0], me, first_weight, second_weight)
    )
    rims = [own_rim] + [over_time(rims[k], k) for k in (1, 2, 3)]
    w1, w2 = call(
        weight_kernel,
        [(3 * C, 9 * C)] * 2,
        [],
        vmem(first_weight.reshape(27, C, C), second_weight.reshape(27, C, C)),
        moved=8 * 27 * C * C,
        name="weights",
    )
    acts, placed = call(
        early_kernel,
        [(FRAMES, C, EXT), (FRAMES, C, PLACED)],
        [
            pltpu.VMEM((FRAMES, C, LANES), jnp.bfloat16),
            pltpu.VMEM((C, 2048), jnp.bfloat16),
            dma((FRAMES,)),
        ],
        smem(me_late) + vmem(first_gain[None]) + anywhere(x, *mains),
        mib=12,
        moved=8 * MIB,
        name="early",
    )
    scales = [a[None] for a in (first_gain, first_bias, second_gain, second_bias)]
    pieces = []
    carry = []
    for first, rows in PARTS:
        common = [w1, w2, *scales]
        outs = block(first, rows, me, exists, placed, carry, [acts, *rims], common)
        own, *carry = lax.optimization_barrier((outs[0], *outs[FRAMES:]))
        pieces.append([own] + [over_time(outs[k], -k) for k in (1, 2, 3)])
    encoded = []
    for (first, rows), part in zip(PARTS, pieces):
        encoded = call(
            functools.partial(place_kernel, first, rows),
            [(C, HT * WT)],
            [dma((FRAMES,))],
            smem(me) + anywhere(*part, *encoded),
            out_space=pl.ANY,
            input_output_aliases={1 + FRAMES: 0} if encoded else {},
            name="place_%d" % first,
        )
    (encoded,) = encoded
    return encoded.reshape(1, 1, C, HT * WT)


def solution(mesh):
    return jax.shard_map(
        on_device,
        mesh=mesh,
        in_specs=(P("tm", "tile", None, None), P(), P(), P(), P(), P(), P()),
        out_specs=P("tm", "tile", None, None),
        check_vma=False,
    )
```
